256 devices in a mesh: dp: 8 (over z), node: 4 (over x), local: 8 (over y, core).
Axes of the slice: x: 4, y: 4, z: 8, core: 2. Of those that a mesh axis runs over, the one named last changes fastest.
Arguments:
- tokens: bfloat16 [65536, 7168], P(('dp', 'node', 'local')), may hold values from -24 to 24
- cotangent: bfloat16 [65536, 7168], P(('dp', 'node', 'local')), may hold values from -24 to 24
- routes: int32 [65536, 8], P(('dp', 'node', 'local')), may hold values from 0 to 383, all different within a row; in each aligned block of 256 rows (0 to 255, 256 to 511, ...) at most 8 rows name the same one
- probs: bfloat16 [65536, 8], P(('dp', 'node', 'local')), may hold values from 0.049804688 to 0.59765625
- w_gate: bfloat16 [4, 7168, 2048], P('node', 'dp', 'local'), may hold values from -0.0625 to 0.0625
- w_up: bfloat16 [4, 7168, 2048], P('node', 'dp', 'local'), may hold values from -0.0625 to 0.0625
- w_down: bfloat16 [4, 2048, 7168], P('node', 'local', 'dp'), may hold values from -0.125 to 0.125
Outputs:
- token_grad: bfloat16 [65536, 7168], P(('dp', 'node', 'local'))
- router_grad: float32 [65536, 8], P(('dp', 'node', 'local'))
- grad_w_gate: bfloat16 [4, 7168, 2048], P('node', 'dp', 'local')
- grad_w_up: bfloat16 [4, 7168, 2048], P('node', 'dp', 'local')
- grad_w_down: bfloat16 [4, 2048, 7168], P('node', 'local', 'dp')
The draws below stay inside these ranges and needn't reach their ends.
Inputs may be any that keep to these rules, and one draw needn't show every extreme that they name: `routes`: each row names 8 different experts; among the rows of one device no expert is named more than 8 times, and in every draw some device names some expert exactly 8 times.
All inputs are finite; a program needn't handle non-finite values.
Results may differ from the reference program's by a relative error of at most 0.017.
Values may be sent and summed in bfloat16 or wider, within the bound.
A program may use at most 192 MiB of HBM per device.

```python
import math
import jax
import jax.numpy as jnp
import numpy as np
from jax import lax

D = 7168
FF = 2048
ROUTED = 384
TOPK = 8
T_DEV = 256
EXPERTS = 4
CAP = 8
TOKENS = 65536
N_DP = 8
N_NODE = 4
N_LOCAL = 8


def raised(entries, rng, source, target, shards_of, factor):
    owner, partner = [(jnp.arange(entries.shape[axis_at]) // (entries.shape[axis_at] // shards_of)).reshape([-1 if axis == axis_at else 1 for axis in range(entries.ndim)]) for axis_at in (source, target)]
    chosen = jax.random.permutation(rng, shards_of)[partner]
    strong = (owner == chosen) | (owner == (partner + shards_of // 2) % shards_of)
    return jnp.where(strong, factor * entries, entries)


def steps_of(rng, shape, cuts, low, high):
    gain, own = 1.0, jax.random.fold_in(rng, 6)
    for axis_at, blocks in cuts:
        draws = jnp.exp(jax.random.uniform(jax.random.fold_in(own, axis_at), (blocks,), jnp.float32, low / len(cuts), high / len(cuts)))
        gain = gain * jnp.repeat(draws, shape[axis_at] // blocks).reshape([-1 if axis == axis_at else 1 for axis in range(len(shape))])
    return gain


def assign_block(rng, own, number, rows, count, top, most, lean):
    sequence = jax.random.permutation(rng, count)
    packed, ordinary = shares(count, rows * top, most, lean, True), shares(count, rows * top, most, lean, False)
    places = jnp.arange(count)

    def named(tallies, rotation):
        used = int((tallies > 0).sum())
        fixed = max(1, used // 4)
        shifted = fixed + (places - fixed + rotation * (used - fixed)) % max(1, count - fixed)
        return jnp.zeros((count,), jnp.int32).at[sequence[jnp.where(places < fixed, places, shifted)]].set(jnp.asarray(tallies, jnp.int32))

    tallies = jnp.where(number % 4 == 0, named(packed, number // 4), named(ordinary, number - number // 4 - 1))
    mixed = jax.random.permutation(jax.random.fold_in(own, 3), count)
    source_of, taker = mixed[0:count // 2 * 2:2], mixed[1:count // 2 * 2:2]
    margin = jnp.minimum(tallies[source_of] - 1, most - tallies[taker]) // 2
    margin = jnp.where((source_of == sequence[0]) | (taker == sequence[0]) | (tallies[taker] == 0), 0, jnp.maximum(margin, 0))
    shifted = jax.random.randint(jax.random.fold_in(own, 4), (count // 2,), 0, 1 << 20) % (margin + 1)
    tallies = tallies.at[source_of].add(-shifted).at[taker].add(shifted)
    items = jnp.searchsorted(jnp.cumsum(tallies), jnp.arange(rows * top), side="right").astype(jnp.int32)
    table = items.reshape(top, rows).T
    table = table[jax.random.permutation(jax.random.fold_in(own, 1), rows)]
    rotation = jax.random.randint(jax.random.fold_in(own, 2), (rows, 1), 0, top)
    return jnp.take_along_axis(table, (jnp.arange(top)[None, :] + rotation) % top, axis=1)


def shares(count, total, bound, lean, full):
    weights = [(1 << 20) // math.isqrt(rank ** lean) + 1 for rank in range(1, count + 1)]
    largest = bound if full else min(bound, max(-(-total // count), total * weights[0] // sum(weights)))
    least = 1 if total - largest >= count - 1 else 0
    counts, surplus = [largest] + [least] * (count - 1), total - largest - least * (count - 1)
    while surplus > 0:
        movable = [i for i in range(1, count) if counts[i] < largest] or [i for i in range(1, count) if counts[i] < bound]
        whole, budget = sum([weights[i] for i in movable]), surplus
        for i in movable:
            addition = min(bound - counts[i], max(1, budget * weights[i] // whole), surplus)
            counts[i] = counts[i] + addition
            surplus = surplus - addition
    return np.array(counts)


def scatter_about(rng, extent, spread, most, pieces=(), kind=jnp.bfloat16):
    factor_of = steps_of(rng, extent, pieces, -0.22, 0.18) if pieces else 1.0
    values = jax.random.normal(rng, extent, jnp.float32) * spread * factor_of
    return jnp.minimum(jnp.maximum(values, -most), most).astype(kind)


def heavy_noise(rng, extent, deviation, reach, shards, heavy, kind=jnp.bfloat16):
    array = deviation * jax.random.normal(rng, extent, jnp.float32)
    if shards:
        array = array * steps_of(rng, extent, shards, -0.22, 0.18)
    return jnp.clip(raised(array, jax.random.fold_in(rng, 3), *heavy), -reach, reach).astype(kind)


def setup_inputs(seed: int = 0) -> dict:
    keys = jax.random.split(jax.random.key(seed), 8)
    tokens = heavy_noise(keys[0], (TOKENS, D), 1.0, 24.0, ((0, 256),), (0, 1, 256, 6.0))
    cotangent = heavy_noise(keys[1], (TOKENS, D), 1.0, 24.0, ((0, 256),), (0, 1, 256, 6.0))
    routes_keys = jax.random.split(jax.random.fold_in(keys[2], 1), TOKENS // T_DEV)
    routes_turns = jax.random.permutation(jax.random.fold_in(keys[2], 3), TOKENS // T_DEV)
    routes = jax.vmap(lambda own, number: assign_block(jax.random.fold_in(keys[2], 2), own, number, T_DEV, ROUTED, TOPK, CAP, 2))(routes_keys, routes_turns).reshape((TOKENS, TOPK))
    probs = jnp.clip(jnp.exp(math.log(0.59765625) - 2.4849066 * jax.random.uniform(keys[3], (TOKENS, TOPK), jnp.float32) ** steps_of(keys[3], (TOKENS, TOPK), ((0, 256),), -0.2, 0.2)), 0.049804688, 0.59765625).astype(jnp.bfloat16)
    w_gate = scatter_about(keys[4], (EXPERTS, D, FF), D ** -0.5, 0.0625, ((0, 4), (1, 8), (2, 8)))
    w_up = scatter_about(keys[5], (EXPERTS, D, FF), D ** -0.5, 0.0625, ((0, 4), (1, 8), (2, 8)))
    w_down = scatter_about(keys[6], (EXPERTS, FF, D), FF ** -0.5, 0.125, ((0, 4), (1, 8), (2, 8)))
    return dict(tokens=tokens, cotangent=cotangent, routes=routes, probs=probs, w_gate=w_gate, w_up=w_up, w_down=w_down)


def slot_positions(route_rows):
    flat_routes = route_rows.reshape(-1).astype(jnp.int32)
    onehot = (flat_routes[:, None] == jnp.arange(EXPERTS, dtype=jnp.int32)[None, :]).astype(jnp.int32)
    earlier = jnp.cumsum(onehot, axis=0) - onehot
    inside = jnp.sum(onehot, axis=1)
    placed = flat_routes * CAP + jnp.sum(earlier * onehot, axis=1)
    return jnp.where(inside > 0, placed, EXPERTS * CAP).astype(jnp.int32)


def pack_tokens(values, positions):
    marks = positions.reshape(T_DEV, TOPK)
    chooser = jnp.sum((marks[None, :, :] == jnp.arange(EXPERTS * CAP, dtype=jnp.int32)[:, None, None]).astype(jnp.int32), axis=2).astype(values.dtype)
    return jnp.dot(chooser, values, preferred_element_type=jnp.float32).astype(values.dtype)


def pack_routes(values, positions):
    chooser = (positions[None, :] == jnp.arange(EXPERTS * CAP, dtype=jnp.int32)[:, None]).astype(values.dtype)
    return jnp.dot(chooser, values, preferred_element_type=jnp.float32).astype(values.dtype)


def rounded(values):
    return lax.optimization_barrier(values.astype(jnp.bfloat16)).astype(jnp.float32)


def expert_terms(rows_in, grads_in, weights_in, gate_slice, up_slice, down_slice):
    gate_value = jnp.dot(rows_in, gate_slice, preferred_element_type=jnp.float32)
    up_value = jnp.dot(rows_in, up_slice, preferred_element_type=jnp.float32)
    sigmoid = jax.nn.sigmoid(gate_value)
    active = gate_value * sigmoid
    hidden = active * up_value
    backed = jnp.dot(grads_in, down_slice.T, preferred_element_type=jnp.float32)
    scales = weights_in.astype(jnp.float32)
    router_part = jnp.sum(backed * hidden, axis=1, keepdims=True)
    grad_hidden = scales * backed
    grad_value = (grad_hidden * active).astype(jnp.bfloat16)
    grad_gate = (grad_hidden * up_value * sigmoid * (1.0 + gate_value * (1.0 - sigmoid))).astype(jnp.bfloat16)
    weighted = (scales * hidden).astype(jnp.bfloat16)
    token_part = jnp.dot(grad_gate, gate_slice.T, preferred_element_type=jnp.float32) + jnp.dot(grad_value, up_slice.T, preferred_element_type=jnp.float32)
    return token_part, router_part, grad_gate, grad_value, weighted


def reference(tokens, cotangent, routes, probs, w_gate, w_up, w_down):
    groups = N_NODE * N_LOCAL
    block_width = FF // N_LOCAL
    token_blocks = tokens.reshape(N_DP, groups, T_DEV, D)
    grad_blocks = cotangent.reshape(N_DP, groups, T_DEV, D)
    route_blocks = routes.reshape(N_DP, groups, T_DEV, TOPK)
    prob_blocks = probs.reshape(N_DP, groups, T_DEV * TOPK, 1)
    gate_slices = w_gate.reshape(EXPERTS, D, N_LOCAL, block_width).transpose(0, 2, 1, 3)
    up_slices = w_up.reshape(EXPERTS, D, N_LOCAL, block_width).transpose(0, 2, 1, 3)
    down_slices = w_down.reshape(EXPERTS, N_LOCAL, block_width, D)

    def to_experts(values):
        return values.reshape(groups, EXPERTS, CAP, -1).transpose(1, 0, 2, 3).reshape(EXPERTS, groups * CAP, -1)

    def to_devices(values):
        table = values.reshape(EXPERTS, groups, CAP, -1).transpose(1, 0, 2, 3).reshape(groups, EXPERTS * CAP, -1)
        return jnp.concatenate([table, jnp.zeros((groups, 1, table.shape[2]), jnp.float32)], axis=1)

    def one_group(totals, item):
        token_rows, grad_rows, route_rows, prob_rows = item
        positions = jax.vmap(slot_positions)(route_rows)
        sent_tokens = to_experts(jax.vmap(pack_tokens)(token_rows, positions))
        sent_grads = to_experts(jax.vmap(pack_tokens)(grad_rows, positions))
        sent_probs = to_experts(jax.vmap(pack_routes)(prob_rows, positions))

        def one_expert(expert_item):
            rows_in, grads_in, weights_in, gate_set, up_set, down_set = expert_item

            def one_slice(slice_item):
                gate_slice, up_slice, down_slice = slice_item
                token_part, router_part, grad_gate, grad_value, weighted = expert_terms(rows_in, grads_in, weights_in, gate_slice, up_slice, down_slice)
                gate_term = jnp.dot(rows_in.T, grad_gate, preferred_element_type=jnp.float32)
                up_term = jnp.dot(rows_in.T, grad_value, preferred_element_type=jnp.float32)
                down_term = jnp.dot(weighted.T, grads_in, preferred_element_type=jnp.float32)
                return rounded(token_part), rounded(router_part), rounded(gate_term), rounded(up_term), rounded(down_term)

            parts = lax.map(one_slice, (gate_set, up_set, down_set))
            return jnp.sum(parts[0], axis=0), jnp.sum(parts[1], axis=0), parts[2], parts[3], parts[4]

        token_sum, router_sum, gate_terms, up_terms, down_terms = lax.map(one_expert, (sent_tokens, sent_grads, sent_probs, gate_slices, up_slices, down_slices))
        token_dev = to_devices(token_sum)
        router_dev = to_devices(router_sum)
        picked_tokens = jax.vmap(lambda source_table, places: source_table[places])(token_dev, positions)
        picked_router = jax.vmap(lambda source_table, places: source_table[places])(router_dev, positions)
        token_grad = jnp.sum(picked_tokens.reshape(groups, T_DEV, TOPK, D), axis=2).astype(jnp.bfloat16)
        router_grad = picked_router.reshape(groups, T_DEV, TOPK)
        totals = (totals[0] + gate_terms, totals[1] + up_terms, totals[2] + down_terms)
        return totals, (token_grad, router_grad)

    start = (jnp.zeros((EXPERTS, N_LOCAL, D, block_width), jnp.float32),
             jnp.zeros((EXPERTS, N_LOCAL, D, block_width), jnp.float32),
             jnp.zeros((EXPERTS, N_LOCAL, block_width, D), jnp.float32))
    totals, outputs = lax.scan(one_group, start, (token_blocks, grad_blocks, route_blocks, prob_blocks))
    grad_w_gate = totals[0].transpose(0, 2, 1, 3).reshape(EXPERTS, D, FF).astype(jnp.bfloat16)
    grad_w_up = totals[1].transpose(0, 2, 1, 3).reshape(EXPERTS, D, FF).astype(jnp.bfloat16)
    grad_w_down = totals[2].reshape(EXPERTS, FF, D).astype(jnp.bfloat16)
    return outputs[0].reshape(TOKENS, D), outputs[1].reshape(TOKENS, TOPK), grad_w_gate, grad_w_up, grad_w_down
```

```python
import functools

import jax
import jax.numpy as jnp
from jax import lax
from jax.experimental import pallas as pl
from jax.experimental.pallas import tpu as pltpu
from jax.sharding import PartitionSpec as P

NZ, NX, NY, NC = 8, 4, 4, 2
CAP = 8
BF = jnp.bfloat16
F32 = jnp.float32
MESH = pl.DeviceIdType.MESH
NN = (((1,), (0,)), ((), ()))
NT = (((1,), (1,)), ((), ()))
TN = (((0,), (0,)), ((), ()))
MIB = 1024 * 1024


def dot(a, b, dims=NN):
    return lax.dot_general(a, b, dims, preferred_element_type=F32)


def choose(routes, probs):
    top, rows = routes.shape
    slots = NX * CAP
    place = lax.broadcasted_iota(jnp.int32, (slots, rows), 0)
    expert = jnp.right_shift(place, 3)
    hit = jnp.zeros((slots, rows), F32)
    scale = jnp.zeros((slots, rows), F32)
    for k in range(top):
        same = routes[k : k + 1, :] == expert
        hit = jnp.where(same, 1.0, hit)
        scale = jnp.where(same, probs[k : k + 1, :], scale)
    before = lax.broadcasted_iota(jnp.int32, (rows, rows), 0) < lax.broadcasted_iota(
        jnp.int32, (rows, rows), 1
    )
    earlier = dot(hit.astype(BF), jnp.where(before, 1.0, 0.0).astype(BF))
    slot = jnp.bitwise_and(place, CAP - 1).astype(F32)
    mark = jnp.where(earlier == slot, hit, 0.0)
    return mark.astype(BF), (mark * scale).astype(BF)


def unpack_kernel(
    routes, probs, choice, table, router, gate_in, up_in, down_in,
    token_grad, router_grad, gate_out, up_out, down_out,
    result, gate_v, up_v, down_v, result_s, load_s, grad_s,
):
    top, rows = routes.shape
    slots = NX * CAP
    width = table.shape[3]
    copies = []

    def copy(src, dst, sem):
        started = pltpu.make_async_copy(src, dst, sem)
        started.start()
        copies.append(started)

    through = ((gate_in, gate_v, gate_out), (up_in, up_v, up_out), (down_in, down_v, down_out))
    loads = [pltpu.make_async_copy(src, v, load_s.at[i]) for i, (src, v, _) in enumerate(through)]
    for load in loads:
        load.start()
    chosen = choice[...]
    for d in range(NZ):
        rows_in = table[d].astype(F32).reshape(slots, width).astype(BF)
        result[d] = dot(chosen, rows_in, TN).astype(BF)
        copy(result.at[d], token_grad.at[:, d * width : (d + 1) * width], result_s.at[d])

    for i, (_, v, dst) in enumerate(through):
        loads[i].wait()
        copy(v, dst.at[0], grad_s.at[i])

    values = (router[0] + router[1] + router[2] + router[3])[0:1, 0:slots]
    row, column = (lax.broadcasted_iota(jnp.int32, (slots, slots), i) for i in range(2))
    values = jnp.sum(jnp.where(row == column, values, 0.0), axis=1, keepdims=True)
    spread = chosen.astype(F32) * values
    expert = jnp.right_shift(lax.broadcasted_iota(jnp.int32, (slots, rows), 0), 3)
    named = routes[...]
    place = lax.broadcasted_iota(jnp.int32, (top, rows), 0)
    total = jnp.zeros((top, rows), F32)
    for k in range(top):
        mine = jnp.where(named[k : k + 1, :] == expert, spread, 0.0)
        total = jnp.where(place == k, jnp.sum(mine, axis=0, keepdims=True), total)
    router_grad[...] = total / probs[...].astype(F32)
    for started in copies:
        started.wait()


def unpack(routes, probs, choice, table, router, gate, lift, drop):
    top, rows = routes.shape
    part = table.shape[3]
    width, ff = gate.shape
    vmem = pl.BlockSpec(memory_space=pltpu.VMEM)
    free = pl.BlockSpec(memory_space=pl.ANY)
    return pl.pallas_call(
        unpack_kernel,
        out_shape=(
            jax.ShapeDtypeStruct((rows, NZ * part), BF),
            jax.ShapeDtypeStruct((top, rows), F32),
            jax.ShapeDtypeStruct((1, width, ff), BF),
            jax.ShapeDtypeStruct((1, width, ff), BF),
            jax.ShapeDtypeStruct((1, ff, width), BF),
        ),
        in_specs=[vmem] * 5 + [free] * 3,
        out_specs=(free, vmem, free, free, free),
        scratch_shapes=[
            pltpu.VMEM((NZ, rows, part), BF),
            pltpu.VMEM((width, ff), BF),
            pltpu.VMEM((width, ff), BF),
            pltpu.VMEM((ff, width), BF),
            pltpu.SemaphoreType.DMA((NZ,)),
            pltpu.SemaphoreType.DMA((3,)),
            pltpu.SemaphoreType.DMA((3,)),
        ],
        compiler_params=pltpu.CompilerParams(vmem_limit_bytes=58 * MIB),
    )(routes, probs, choice, table, router, gate, lift, drop)


GROUP_Y = (0, 1, NY - 1, 2)
ORDER = (0, 1, 3, 2)

GAP = 8
STAGES = (
    ("take", 0), ("pass_on", 5), ("near", 7), ("far", 10),
    ("products", 13), ("scatter_1", 17), ("scatter_2", 21), ("scatter_3", 25),
    ("hidden", 29), ("gather_1", 33), ("gather_2", 37), ("gather_3", 41),
    ("tokens", 45), ("weights", 46), ("join", 49), ("relay", 52), ("finish", 55),
)


def expert_kernel(
    routes, probs, tokens_in, cotangent_in, gate_in, up_in, down_in,
    choice, table, router, grad_gate_out, grad_up_out, grad_down_out,
    tokens_v, cotangent_v, w_gate, w_up, w_down, grad_gate, grad_up, grad_down, packed,
    land, rows, part, minus, plus, grads, tokens_out, sibling_in, near_in, far_in, final,
    acc_gate, acc_up, acc_down, tile_z, tile_zin, tile, tile_in, tile_x,
    a2a_s, a2a_r, y_s, y_r, sib_s, sib_r, rs_s, rs_r, ag_s, ag_r, t_s, t_r, yr_s, yr_r,
    back_s, back_r, in_s, w_s, out_s, r0_s, r0_r, r1_s, r1_r, r2_s, r2_r,
):
    z, x, loc = lax.axis_index("dp"), lax.axis_index("node"), lax.axis_index("local")
    y, c = loc // NC, loc % NC
    width = packed.shape[3]
    ff = w_gate.shape[1]
    block = NZ * CAP
    count = NC * NY * block

    def at(dz=0, dx=0, dy=0, dc=0):
        return {
            "dp": (z + dz) % NZ,
            "node": (x + dx) % NX,
            "local": ((y + dy) % NY) * NC + (c + dc) % NC,
        }

    steps_z = (4, 3, 5, 2, 6, 1, 7, 0)
    loads = []
    for dz in steps_z:
        start = pl.multiple_of((z + dz) % NZ * width, 128)
        for i, (src, dst) in enumerate(((tokens_in, tokens_v), (cotangent_in, cotangent_v))):
            load = pltpu.make_async_copy(src.at[:, pl.ds(start, width)], dst.at[dz], in_s.at[i, dz])
            load.start()
            loads.append(load)
    weight_loads = [
        pltpu.make_async_copy(src, dst, w_s.at[i])
        for i, (src, dst) in enumerate(((gate_in, w_gate), (up_in, w_up), (down_in, w_down)))
    ]
    for load in weight_loads:
        load.start()

    sends = []

    def send(src, dst, send_sem, recv_sem, device):
        copy = pltpu.make_async_remote_copy(
            src_ref=src, dst_ref=dst, send_sem=send_sem, recv_sem=recv_sem,
            device_id=device, device_id_type=MESH,
        )
        copy.start()
        sends.append(copy)

    def arrived(dst, recv_sem, device):
        pltpu.make_async_remote_copy(
            src_ref=dst, dst_ref=dst, send_sem=recv_sem, recv_sem=recv_sem,
            device_id=device, device_id_type=MESH,
        ).wait_recv()

    def add(a, b):
        return (a.astype(F32) + b.astype(F32)).astype(BF)

    plane = [(dz, p) for p in ORDER for dz in steps_z if (dz, p) != (0, 0)]
    around = [(k, g) for k in range(NC) for g in range(NY) if (k, g) != (0, 0)]

    barrier = pltpu.get_barrier_semaphore()
    for dz, dx in plane:
        pl.semaphore_signal(barrier, inc=1, device_id=at(dz, dx), device_id_type=MESH)
    for k, g in around:
        pl.semaphore_signal(barrier, inc=1, device_id=at(dy=GROUP_Y[g], dc=k), device_id_type=MESH)
    pick, pick_scaled = choose(routes[...], probs[...].astype(F32))
    choice[...] = pick
    pl.semaphore_wait(barrier, len(plane) + len(around))

    def give(dz, p):
        if (dz, p) == (0, 0):
            land[0, z] = packed[0, x]
            return
        dx, back = (-p) % NX, (-dz) % NZ
        send(
            packed.at[dz, (x + dx) % NX], land.at[p, z],
            a2a_s.at[p, dz], a2a_r.at[p, back], at(dz, dx),
        )

    for i, dz in enumerate(steps_z):
        loads[2 * i].wait()
        loads[2 * i + 1].wait()
        rows_x = dot(pick, tokens_v[dz]).reshape(NX, CAP, width)
        rows_c = dot(pick_scaled, cotangent_v[dz]).reshape(NX, CAP, width)
        packed[dz] = jnp.concatenate([rows_x, rows_c], axis=1).astype(BF)
        give(dz, ORDER[0])
    for p in ORDER[1:]:
        for dz in steps_z:
            give(dz, p)
    for load in weight_loads:
        load.wait()

    up, down, other = at(dy=1), at(dy=NY - 1), at(dc=1)
    zup, zdown = at(dz=1), at(dz=NZ - 1)

    def take(p):
        for dz in range(NZ):
            if (dz, p) != (0, 0):
                arrived(land.at[p, (z + dz) % NZ], a2a_r.at[p, dz], at(dz, p))
        mixed = land[p].astype(F32)
        rows[p, 0, 0, 0] = mixed[:, :CAP].reshape(block, width).astype(BF)
        rows[p, 1, 0, 0] = mixed[:, CAP:].reshape(block, width).astype(BF)
        for h in range(2):
            send(rows.at[p, h, 0, 0], rows.at[p, h, 0, 1], y_s.at[p, 1, h], y_r.at[p, 1, h], down)
            send(
                rows.at[p, 1 - h, 0, 0], rows.at[p, 1 - h, 0, 2],
                y_s.at[p, 2, 1 - h], y_r.at[p, 2, 1 - h], up,
            )
        for h in range(2):
            to_sibling(p, 0, h)

    def to_sibling(p, g, h):
        send(rows.at[p, h, 0, g], rows.at[p, h, 1, g], sib_s.at[p, g, h], sib_r.at[p, g, h], other)

    def from_y(p, g, h):
        arrived(rows.at[p, h, 0, g], y_r.at[p, g, h], up)

    def pass_on(p):
        from_y(p, 1, 0)
        send(rows.at[p, 0, 0, 1], rows.at[p, 0, 0, 3], y_s.at[p, 3, 0], y_r.at[p, 3, 0], down)
        from_y(p, 2, 1)
        send(rows.at[p, 1, 0, 2], rows.at[p, 1, 0, 3], y_s.at[p, 3, 1], y_r.at[p, 3, 1], up)
        to_sibling(p, 1, 0)
        to_sibling(p, 2, 1)

    def near(p):
        from_y(p, 1, 1)
        to_sibling(p, 1, 1)
        from_y(p, 2, 0)
        to_sibling(p, 2, 0)

    def far(p):
        for h in range(2):
            from_y(p, 3, h)
            to_sibling(p, 3, h)

    def products(p):
        for g in range(NY):
            for h in range(2):
                arrived(rows.at[p, h, 1, g], sib_r.at[p, g, h], other)
        in_rows = rows[p, 0].reshape(count, width)
        in_grads = rows[p, 1].reshape(count, width)
        shape = (NZ, block, ff)
        part[p, :, :, 0:ff] = dot(in_rows, w_gate[...]).astype(BF).reshape(shape)
        part[p, :, :, ff : 2 * ff] = dot(in_rows, w_up[...]).astype(BF).reshape(shape)
        part[p, :, :, 2 * ff :] = dot(in_grads, w_down[...], NT).astype(BF).reshape(shape)
        goal = (z + 4) % NZ
        half = block // 2
        send(
            part.at[p, goal, 0:half], minus.at[p, 0, 0:half], rs_s.at[p, 0, 0], rs_r.at[p, 0, 0], zdown
        )
        send(part.at[p, goal, half:], plus.at[p, 0, half:], rs_s.at[p, 1, 0], rs_r.at[p, 1, 0], zup)

    def scatter(p, s):
        low, high = (z + 4 + s) % NZ, (z + 4 - s) % NZ
        half = block // 2
        if s == 1:
            arrived(minus.at[p, 0, 0:half], rs_r.at[p, 0, 0], zup)
            part[p, low, 0:half] = add(part[p, low, 0:half], minus[p, 0, 0:half])
        else:
            arrived(minus.at[p, s - 1], rs_r.at[p, 0, s - 1], zup)
            part[p, low] = add(part[p, low], minus[p, s - 1])
        send(part.at[p, low], minus.at[p, s], rs_s.at[p, 0, s], rs_r.at[p, 0, s], zdown)
        if s == 1:
            arrived(plus.at[p, 0, half:], rs_r.at[p, 1, 0], zdown)
            part[p, high, half:] = add(part[p, high, half:], plus[p, 0, half:])
        else:
            arrived(plus.at[p, s - 1], rs_r.at[p, 1, s - 1], zdown)
            part[p, high] = add(part[p, high], plus[p, s - 1])
        send(part.at[p, high], plus.at[p, s], rs_s.at[p, 1, s], rs_r.at[p, 1, s], zup)

    def hidden(p):
        arrived(minus.at[p, 3], rs_r.at[p, 0, 3], zup)
        arrived(plus.at[p, 3], rs_r.at[p, 1, 3], zdown)
        total = part[p, z].astype(F32) + minus[p, 3].astype(F32) + plus[p, 3].astype(F32)
        gate, lift, back = total[:, :ff], total[:, ff : 2 * ff], total[:, 2 * ff :]
        sigmoid = 1.0 / (1.0 + jnp.exp(-gate))
        active = gate * sigmoid
        value = active * lift
        mine = grads.at[p, z]
        mine[:, 0:ff] = (back * lift * sigmoid * (1.0 + gate * (1.0 - sigmoid))).astype(BF)
        mine[:, ff : 2 * ff] = (back * active).astype(BF)
        mine[:, 2 * ff :] = value.astype(BF)
        send(mine, mine, ag_s.at[p, 1, 0], ag_r.at[p, 1, 0], zup)
        send(mine, mine, ag_s.at[p, 0, 0], ag_r.at[p, 0, 0], zdown)
        terms = back * value
        high = terms.astype(BF)
        rest = (terms - high.astype(F32)).astype(BF)
        ones = jnp.ones((8, ff), BF)
        summed = dot(ones, high, NT) + dot(ones, rest, NT)
        tile_z[p : p + 1, 0:block] = summed[0:1]

    def gather(p, s):
        low, high = grads.at[p, (z + s) % NZ], grads.at[p, (z - s + NZ) % NZ]
        half = block // 2
        arrived(low, ag_r.at[p, 0, s - 1], zup)
        if s < 3:
            send(low, low, ag_s.at[p, 0, s], ag_r.at[p, 0, s], zdown)
        else:
            first = grads.at[p, (z + s) % NZ, 0:half]
            send(first, first, ag_s.at[p, 0, s], ag_r.at[p, 0, s], zdown)
        arrived(high, ag_r.at[p, 1, s - 1], zdown)
        if s < 3:
            send(high, high, ag_s.at[p, 1, s], ag_r.at[p, 1, s], zup)
        else:
            last = grads.at[p, (z - s + NZ) % NZ, half:]
            send(last, last, ag_s.at[p, 1, s], ag_r.at[p, 1, s], zup)

    def tokens(p):
        half = block // 2
        arrived(grads.at[p, (z + 4) % NZ, 0:half], ag_r.at[p, 0, 3], zup)
        arrived(grads.at[p, (z + 4) % NZ, half:], ag_r.at[p, 1, 3], zdown)
        for k in (1, 0):
            both = grads[p, k * NY : (k + 1) * NY].reshape(NY * block, 3 * ff)
            value = dot(both[:, :ff], w_gate[...], NT) + dot(both[:, ff : 2 * ff], w_up[...], NT)
            tokens_out[p, k] = value.astype(BF).reshape(NY, block, width)
            if k == 1:
                send(tokens_out.at[p, 1], sibling_in.at[p], t_s.at[p], t_r.at[p], other)

    stores = [
        pltpu.make_async_copy(src, dst, out_s.at[i])
        for i, (src, dst) in enumerate(
            ((grad_gate, grad_gate_out), (grad_up, grad_up_out), (grad_down, grad_down_out))
        )
    ]

    def weights(p):
        both = grads[p].reshape(count, 3 * ff)
        in_rows = rows[p, 0].reshape(count, width)
        in_grads = rows[p, 1].reshape(count, width)
        gate = dot(in_rows, both[:, :ff], TN)
        lift = dot(in_rows, both[:, ff : 2 * ff], TN)
        drop = dot(both[:, 2 * ff :], in_grads, TN)
        if p == ORDER[0]:
            acc_gate[...], acc_up[...], acc_down[...] = gate, lift, drop
        elif p != ORDER[-1]:
            acc_gate[...] += gate
            acc_up[...] += lift
            acc_down[...] += drop
        else:
            grad_gate[...] = (acc_gate[...] + gate).astype(BF)
            grad_up[...] = (acc_up[...] + lift).astype(BF)
            grad_down[...] = (acc_down[...] + drop).astype(BF)
            for copy in stores:
                copy.start()

    def join(p):
        half = block // 2
        arrived(sibling_in.at[p], t_r.at[p], other)
        tokens_out[p, 0] = add(tokens_out[p, 0], sibling_in[p])
        send(tokens_out.at[p, 0, 3, 0:half], far_in.at[p, 0], yr_s.at[p, 0], yr_r.at[p, 0], up)
        send(tokens_out.at[p, 0, 3, half:], far_in.at[p, 1], yr_s.at[p, 1], yr_r.at[p, 1], down)

    def relay(p):
        half = block // 2
        arrived(far_in.at[p, 0], yr_r.at[p, 0], down)
        tokens_out[p, 0, 1, 0:half] = add(tokens_out[p, 0, 1, 0:half], far_in[p, 0])
        send(tokens_out.at[p, 0, 1], near_in.at[p, 0], yr_s.at[p, 2], yr_r.at[p, 2], up)
        arrived(far_in.at[p, 1], yr_r.at[p, 1], up)
        tokens_out[p, 0, 2, half:] = add(tokens_out[p, 0, 2, half:], far_in[p, 1])
        send(tokens_out.at[p, 0, 2], near_in.at[p, 1], yr_s.at[p, 3], yr_r.at[p, 3], down)

    def finish(p):
        arrived(near_in.at[p, 0], yr_r.at[p, 2], down)
        arrived(near_in.at[p, 1], yr_r.at[p, 3], up)
        value = tokens_out[p, 0, 0].astype(F32) + near_in[p, 0].astype(F32) + near_in[p, 1].astype(F32)
        final[p] = value.reshape(NZ, CAP, width).astype(BF)
        for dz in steps_z:
            if (dz, p) != (0, 0):
                send(
                    final.at[p, (z + dz) % NZ], table.at[z, x],
                    back_s.at[p, dz], back_r.at[(-p) % NX, (-dz) % NZ], at(dz, p),
                )
            else:
                table[z, x] = final[p, z]

    others_z = range(1, NZ)

    def router_start():
        for dz in others_z:
            send(tile_z, tile_zin.at[z], r0_s.at[dz], r0_r.at[(-dz) % NZ], at(dz))
        tile_zin[z] = tile_z[...]

    def three_parts(value):
        top = value.astype(BF)
        middle = (value - top.astype(F32)).astype(BF)
        low = (value - top.astype(F32) - middle.astype(F32)).astype(BF)
        return top, middle, low

    def moved(value, source, goal):
        move = jnp.where(source & goal, 1.0, 0.0).astype(BF)
        top, middle, low = three_parts(value)
        return dot(top, move) + dot(middle, move) + dot(low, move)

    row = lax.broadcasted_iota(jnp.int32, (128, 128), 0)
    column = lax.broadcasted_iota(jnp.int32, (128, 128), 1)
    in_slot = jnp.bitwise_and(row, CAP - 1)

    def router_local():
        for dz in others_z:
            arrived(tile_zin.at[(z + dz) % NZ], r0_r.at[dz], at(dz))
        total = jnp.zeros((8, 128), F32)
        inside = lax.broadcasted_iota(jnp.int32, (8, 128), 1) < block
        for p in range(NX):
            value = jnp.concatenate([tile_zin[b, p : p + 1, :] for b in range(NZ)], axis=0)
            value = jnp.where(inside, value, 0.0)
            total = total + moved(value, jnp.right_shift(row, 3) == z, column == p * CAP + in_slot)
        tile[...] = total
        for k, g in around:
            i = NY * k + g
            send(tile, tile_in.at[i], r1_s.at[i], r1_r.at[i], at(dy=GROUP_Y[g], dc=k))

    def router_x():
        summed = tile[0:1, :]
        for k, g in around:
            i = NY * k + g
            arrived(tile_in.at[i], r1_r.at[i], other)
            summed = summed + tile_in[i, i : i + 1, :]
        wide = jnp.broadcast_to(summed, (8, 128))
        for dx in range(NX):
            tile_x[dx] = moved(wide, jnp.right_shift(row, 3) == dx, column == x * CAP + in_slot)
        router[x] = tile_x[0]
        for dx in range(1, NX):
            send(tile_x.at[dx], router.at[x], r2_s.at[dx], r2_r.at[(-dx) % NX], at(dx=dx))

    todo = {
        "take": take, "pass_on": pass_on, "near": near, "far": far, "products": products,
        "hidden": hidden, "tokens": tokens, "weights": weights, "join": join, "relay": relay,
        "finish": finish,
    }
    for s in (1, 2, 3):
        todo[f"scatter_{s}"] = functools.partial(scatter, s=s)
        todo[f"gather_{s}"] = functools.partial(gather, s=s)
    plan = [
        (start + place * GAP, place, stage, p)
        for place, p in enumerate(ORDER)
        for stage, start in STAGES
    ]
    last = {stage: start + (NX - 1) * GAP for stage, start in STAGES}
    plan.append((last["hidden"] + 0.1, NX, router_start, None))
    plan.append((last["gather_2"] + 0.1, NX, router_local, None))
    plan.append((last["tokens"] + 0.1, NX, router_x, None))
    for _, _, stage, p in sorted(plan, key=lambda item: item[:2]):
        if p is None:
            stage()
        else:
            todo[stage](p)

    for dx in range(1, NX):
        arrived(router.at[(x + dx) % NX], r2_r.at[dx], at(dx=dx))
    for p in ORDER:
        for dz in range(NZ):
            if (dz, p) != (0, 0):
                arrived(table.at[(z + dz) % NZ, (x + p) % NX], back_r.at[p, dz], at(dz, p))
    for copy in stores:
        copy.wait()
    for copy in sends:
        copy.wait_send()


def experts(routes, probs, tokens, cotangent, w_gate, w_up, w_down):
    width, ff = w_gate.shape
    count = tokens.shape[0]
    block = NZ * CAP
    vmem = pl.BlockSpec(memory_space=pltpu.VMEM)
    free = pl.BlockSpec(memory_space=pl.ANY)
    dma = lambda *shape: pltpu.SemaphoreType.DMA(shape)
    flops = 2 * 8 * NX * NC * NY * block * width * ff
    return pl.pallas_call(
        expert_kernel,
        out_shape=(
            jax.ShapeDtypeStruct((NX * CAP, count), BF),
            jax.ShapeDtypeStruct((NZ, NX, CAP, width), BF),
            jax.ShapeDtypeStruct((NX, 8, 128), F32),
            jax.ShapeDtypeStruct((width, ff), BF),
            jax.ShapeDtypeStruct((width, ff), BF),
            jax.ShapeDtypeStruct((ff, width), BF),
        ),
        in_specs=[vmem] * 2 + [free] * 5,
        out_specs=(vmem,) * 3 + (free,) * 3,
        scratch_shapes=[
            pltpu.VMEM((NZ, count, width), BF),
            pltpu.VMEM((NZ, count, width), BF),
            pltpu.VMEM((width, ff), BF),
            pltpu.VMEM((width, ff), BF),
            pltpu.VMEM((ff, width), BF),
            pltpu.VMEM((width, ff), BF),
            pltpu.VMEM((width, ff), BF),
            pltpu.VMEM((ff, width), BF),
            pltpu.VMEM((NZ, NX, 2 * CAP, width), BF),
            pltpu.VMEM((NX, NZ, 2 * CAP, width), BF),
            pltpu.VMEM((NX, 2, NC, NY, block, width), BF),
            pltpu.VMEM((NX, NZ, block, 3 * ff), BF),
            pltpu.VMEM((NX, 4, block, 3 * ff), BF),
            pltpu.VMEM((NX, 4, block, 3 * ff), BF),
            pltpu.VMEM((NX, NZ, block, 3 * ff), BF),
            pltpu.VMEM((NX, NC, NY, block, width), BF),
            pltpu.VMEM((NX, NY, block, width), BF),
            pltpu.VMEM((NX, 2, block, width), BF),
            pltpu.VMEM((NX, 2, block // 2, width), BF),
            pltpu.VMEM((NX, NZ, CAP, width), BF),
            pltpu.VMEM((width, ff), F32),
            pltpu.VMEM((width, ff), F32),
            pltpu.VMEM((ff, width), F32),
            pltpu.VMEM((8, 128), F32),
            pltpu.VMEM((NZ, 8, 128), F32),
            pltpu.VMEM((8, 128), F32),
            pltpu.VMEM((8, 8, 128), F32),
            pltpu.VMEM((NX, 8, 128), F32),
            dma(NX, NZ), dma(NX, NZ), dma(NX, NY, 2), dma(NX, NY, 2), dma(NX, NY, 2), dma(NX, NY, 2),
            dma(NX, 2, 4), dma(NX, 2, 4), dma(NX, 2, 4), dma(NX, 2, 4),
            dma(NX), dma(NX), dma(NX, 4), dma(NX, 4),
            dma(NX, NZ), dma(NX, NZ), dma(2, NZ), dma(3), dma(3), dma(NZ), dma(NZ), dma(8), dma(8), dma(NX), dma(NX),
        ],
        compiler_params=pltpu.CompilerParams(
            collective_id=0, has_side_effects=True, vmem_limit_bytes=56 * MIB
        ),
        cost_estimate=pl.CostEstimate(flops=flops, bytes_accessed=16 * MIB, transcendentals=0),
    )(routes, probs, tokens, cotangent, w_gate, w_up, w_down)


def per_device(tokens, cotangent, routes, probs, w_gate, w_up, w_down):
    routes, probs = routes.T, probs.T
    choice, table, router, gate, lift, drop = experts(
        routes, probs, tokens, cotangent, w_gate[0], w_up[0], w_down[0]
    )
    token_grad, router_grad, gate, lift, drop = unpack(
        routes, probs, choice, table, router, gate, lift, drop
    )
    return token_grad, router_grad.T, gate, lift, drop


def solution(mesh):
    split = P(("dp", "node", "local"), None)
    specs = (P("node", "dp", "local"), P("node", "dp", "local"), P("node", "local", "dp"))
    return jax.shard_map(
        per_device,
        mesh=mesh,
        in_specs=(split,) * 4 + specs,
        out_specs=(split,) * 2 + specs,
        check_vma=False,
    )
```

```python
import functools

import jax
import jax.numpy as jnp
from jax import lax
from jax.experimental import pallas as pl
from jax.experimental.pallas import tpu as pltpu
from jax.sharding import PartitionSpec as P

NZ, NX, NY, NC = 8, 4, 4, 2
CAP = 8
BF = jnp.bfloat16
F32 = jnp.float32
MESH = pl.DeviceIdType.MESH
NN = (((1,), (0,)), ((), ()))
NT = (((1,), (1,)), ((), ()))
TN = (((0,), (0,)), ((), ()))
MIB = 1024 * 1024


def dot(a, b, dims=NN):
    return lax.dot_general(a, b, dims, preferred_element_type=F32)


def choose(routes, probs):
    top, rows = routes.shape
    slots = NX * CAP
    place = lax.broadcasted_iota(jnp.int32, (slots, rows), 0)
    expert = jnp.right_shift(place, 3)
    hit = jnp.zeros((slots, rows), F32)
    scale = jnp.zeros((slots, rows), F32)
    for k in range(top):
        same = routes[k : k + 1, :] == expert
        hit = jnp.where(same, 1.0, hit)
        scale = jnp.where(same, probs[k : k + 1, :], scale)
    before = lax.broadcasted_iota(jnp.int32, (rows, rows), 0) < lax.broadcasted_iota(
        jnp.int32, (rows, rows), 1
    )
    earlier = dot(hit.astype(BF), jnp.where(before, 1.0, 0.0).astype(BF))
    slot = jnp.bitwise_and(place, CAP - 1).astype(F32)
    mark = jnp.where(earlier == slot, hit, 0.0)
    return mark.astype(BF), (mark * scale).astype(BF)


def unpack_kernel(
    routes, probs, choice, table, router, gate_in, up_in, down_in,
    token_grad, router_grad, gate_out, up_out, down_out,
    result, gate_v, up_v, down_v, result_s, load_s, grad_s,
):
    top, rows = routes.shape
    slots = NX * CAP
    width = table.shape[3]
    copies = []

    def copy(src, dst, sem):
        started = pltpu.make_async_copy(src, dst, sem)
        started.start()
        copies.append(started)

    through = ((gate_in, gate_v, gate_out), (up_in, up_v, up_out), (down_in, down_v, down_out))
    loads = [pltpu.make_async_copy(src, v, load_s.at[i]) for i, (src, v, _) in enumerate(through)]
    for load in loads:
        load.start()
    chosen = choice[...]
    for d in range(NZ):
        rows_in = table[d].astype(F32).reshape(slots, width).astype(BF)
        result[d] = dot(chosen, rows_in, TN).astype(BF)
        copy(result.at[d], token_grad.at[:, d * width : (d + 1) * width], result_s.at[d])

    for i, (_, v, dst) in enumerate(through):
        loads[i].wait()
        copy(v, dst.at[0], grad_s.at[i])

    values = (router[0] + router[1] + router[2] + router[3])[0:1, 0:slots]
    row, column = (lax.broadcasted_iota(jnp.int32, (slots, slots), i) for i in range(2))
    values = jnp.sum(jnp.where(row == column, values, 0.0), axis=1, keepdims=True)
    spread = chosen.astype(F32) * values
    expert = jnp.right_shift(lax.broadcasted_iota(jnp.int32, (slots, rows), 0), 3)
    named = routes[...]
    place = lax.broadcasted_iota(jnp.int32, (top, rows), 0)
    total = jnp.zeros((top, rows), F32)
    for k in range(top):
        mine = jnp.where(named[k : k + 1, :] == expert, spread, 0.0)
        total = jnp.where(place == k, jnp.sum(mine, axis=0, keepdims=True), total)
    router_grad[...] = total / probs[...].astype(F32)
    for started in copies:
        started.wait()


def unpack(routes, probs, choice, table, router, gate, lift, drop):
    top, rows = routes.shape
    part = table.shape[3]
    width, ff = gate.shape
    vmem = pl.BlockSpec(memory_space=pltpu.VMEM)
    free = pl.BlockSpec(memory_space=pl.ANY)
    return pl.pallas_call(
        unpack_kernel,
        out_shape=(
            jax.ShapeDtypeStruct((rows, NZ * part), BF),
            jax.ShapeDtypeStruct((top, rows), F32),
            jax.ShapeDtypeStruct((1, width, ff), BF),
            jax.ShapeDtypeStruct((1, width, ff), BF),
            jax.ShapeDtypeStruct((1, ff, width), BF),
        ),
        in_specs=[vmem] * 5 + [free] * 3,
        out_specs=(free, vmem, free, free, free),
        scratch_shapes=[
            pltpu.VMEM((NZ, rows, part), BF),
            pltpu.VMEM((width, ff), BF),
            pltpu.VMEM((width, ff), BF),
            pltpu.VMEM((ff, width), BF),
            pltpu.SemaphoreType.DMA((NZ,)),
            pltpu.SemaphoreType.DMA((3,)),
            pltpu.SemaphoreType.DMA((3,)),
        ],
        compiler_params=pltpu.CompilerParams(vmem_limit_bytes=58 * MIB),
    )(routes, probs, choice, table, router, gate, lift, drop)


GROUP_Y = (0, 1, NY - 1, 2)
ORDER = (0, 1, 3, 2)

STAGES = (
    ("take", 0, 3, 13, 23),
    ("pass_tokens", 1, 9, 19, 34),
    ("pass_grads", 2, 10, 22, 35),
    ("near_grads", 5, 11, 24, 46),
    ("near_tokens", 4, 12, 27, 38),
    ("far_tokens", 6, 16, 31, 41),
    ("far_grads", 7, 17, 30, 42),
    ("products", 8, 18, 36, 48),
    ("scatter_down_1", 14, 25, 43, 52),
    ("scatter_up_1", 15, 26, 44, 56),
    ("scatter_down_2", 21, 32, 53, 59),
    ("scatter_up_2", 20, 33, 54, 62),
    ("scatter_down_3", 28, 39, 61, 65),
    ("scatter_up_3", 29, 40, 60, 67),
    ("hidden", 37, 49, 68, 73),
    ("gather_down_1", 45, 55, 74, 77),
    ("gather_up_1", 47, 58, 75, 78),
    ("gather_down_2", 50, 63, 81, 83),
    ("gather_up_2", 51, 64, 82, 84),
    ("gather_down_3", 57, 70, 87, 91),
    ("gather_up_3", 66, 71, 89, 92),
    ("tokens", 72, 76, 93, 94),
    ("weights", 69, 104, 106, 107),
    ("join", 80, 79, 95, 97),
    ("relay_up", 85, 88, 98, 102),
    ("relay_down", 86, 90, 99, 101),
    ("finish", 96, 100, 103, 105),
)


def expert_kernel(
    routes, probs, tokens_in, cotangent_in, gate_in, up_in, down_in,
    choice, table, router, grad_gate_out, grad_up_out, grad_down_out,
    inputs, w_gate, w_up, w_down, grad_gate, grad_up, grad_down, packed,
    land, rows, part, minus, plus, grads, tokens_out, sibling_in, near_in, far_in, final,
    acc_gate, acc_up, acc_down, tile_z, tile_zin, tile, tile_in, tile_x,
    sent, a2a_r, y_r, sib_r, rs_r, ag_r, t_r, yr_r, back_r, in_s, w_s, out_s, router_r,
):
    z, x, loc = lax.axis_index("dp"), lax.axis_index("node"), lax.axis_index("local")
    y, c = loc // NC, loc % NC
    width = packed.shape[2]
    ff = w_gate.shape[1]
    block = NZ * CAP
    count = NC * NY * block

    def at(dz=0, dx=0, dy=0, dc=0):
        return {
            "dp": (z + dz) % NZ,
            "node": (x + dx) % NX,
            "local": ((y + dy) % NY) * NC + (c + dc) % NC,
        }

    steps_z = (4, 3, 5, 2, 6, 1, 7, 0)
    for dz in steps_z:
        start = pl.multiple_of((z + dz) % NZ * width, 128)
        for i, src in enumerate((tokens_in, cotangent_in)):
            pltpu.make_async_copy(
                src.at[:, pl.ds(start, width)], inputs.at[dz, i], in_s.at[dz]
            ).start()
    weight_loads = [
        pltpu.make_async_copy(src, dst, w_s.at[i])
        for i, (src, dst) in enumerate(((gate_in, w_gate), (up_in, w_up), (down_in, w_down)))
    ]
    for load in weight_loads:
        load.start()

    kinds = ("a2a", "y", "sibling", "scatter", "gather", "terms", "sums", "back", "rz", "ry", "rx")

    def send(src, dst, kind, recv_sem, device):
        pltpu.make_async_remote_copy(
            src_ref=src, dst_ref=dst, send_sem=sent.at[kinds.index(kind)], recv_sem=recv_sem,
            device_id=device, device_id_type=MESH,
        ).start()

    def all_sent(kind, same_bytes):
        pltpu.make_async_remote_copy(
            src_ref=same_bytes, dst_ref=same_bytes, send_sem=sent.at[kinds.index(kind)],
            recv_sem=back_r, device_id=at(dz=1), device_id_type=MESH,
        ).wait_send()

    def arrived(dst, recv_sem, device):
        pltpu.make_async_remote_copy(
            src_ref=dst, dst_ref=dst, send_sem=recv_sem, recv_sem=recv_sem,
            device_id=device, device_id_type=MESH,
        ).wait_recv()

    def add(a, b):
        return (a.astype(F32) + b.astype(F32)).astype(BF)

    plane = [(dz, p) for p in ORDER for dz in steps_z if (dz, p) != (0, 0)]
    around = [(k, g) for k in range(NC) for g in range(NY) if (k, g) != (0, 0)]

    barrier = pltpu.get_barrier_semaphore()
    for dz, dx in plane:
        pl.semaphore_signal(barrier, inc=1, device_id=at(dz, dx), device_id_type=MESH)
    for k, g in around:
        pl.semaphore_signal(barrier, inc=1, device_id=at(dy=GROUP_Y[g], dc=k), device_id_type=MESH)
    pick, pick_scaled = choose(routes[...], probs[...].astype(F32))
    choice[...] = pick
    pl.semaphore_wait(barrier, len(plane) + len(around))

    def give(dz, p):
        if (dz, p) == (0, 0):
            land[0, z] = packed[x]
            return
        dx = (-p) % NX
        send(packed.at[dz * NX + (x + dx) % NX], land.at[p, z], "a2a", a2a_r.at[p], at(dz, dx))

    for dz in steps_z:
        pltpu.make_async_copy(inputs.at[dz], inputs.at[dz], in_s.at[dz]).wait()
        rows_x = dot(pick, inputs[dz, 0]).reshape(NX, CAP, width)
        rows_c = dot(pick_scaled, inputs[dz, 1]).reshape(NX, CAP, width)
        packed[dz * NX : (dz + 1) * NX] = jnp.concatenate([rows_x, rows_c], axis=1).astype(BF)
        give(dz, ORDER[0])
    for p in ORDER[1:]:
        for dz in steps_z:
            give(dz, p)
    for load in weight_loads:
        load.wait()

    up, down, other = at(dy=1), at(dy=NY - 1), at(dc=1)
    zup, zdown = at(dz=1), at(dz=NZ - 1)

    def take(p):
        arrived(land.at[p, (1 if p == 0 else 0) : NZ], a2a_r.at[p], zup)
        mixed = land[p].astype(F32)
        rows[p, 0, 0, 0] = mixed[:, :CAP].reshape(block, width).astype(BF)
        rows[p, 1, 0, 0] = mixed[:, CAP:].reshape(block, width).astype(BF)
        for h in range(2):
            send(rows.at[p, h, 0, 0], rows.at[p, h, 0, 1], "y", y_r.at[p, 0, h], down)
            send(rows.at[p, 1 - h, 0, 0], rows.at[p, 1 - h, 0, 2], "y", y_r.at[p, 1, 1 - h], up)
        for h in range(2):
            to_sibling(p, 0, h)

    def to_sibling(p, g, h):
        send(rows.at[p, h, 0, g], rows.at[p, h, 1, g], "sibling", sib_r.at[p], other)

    def from_y(p, g, h):
        arrived(rows.at[p, h, 0, g], y_r.at[p, g - 1, h], up)

    def pass_tokens(p):
        from_y(p, 1, 0)
        send(rows.at[p, 0, 0, 1], rows.at[p, 0, 0, 3], "y", y_r.at[p, 2, 0], down)
        to_sibling(p, 1, 0)

    def pass_grads(p):
        from_y(p, 2, 1)
        send(rows.at[p, 1, 0, 2], rows.at[p, 1, 0, 3], "y", y_r.at[p, 2, 1], up)
        to_sibling(p, 2, 1)

    def keep(p, g, h):
        from_y(p, g, h)
        to_sibling(p, g, h)

    def products(p):
        arrived(rows.at[p, :, 1], sib_r.at[p], other)
        in_rows = rows[p, 0].reshape(count, width)
        in_grads = rows[p, 1].reshape(count, width)
        shape = (NZ, block, ff)
        part[p, :, :, 0:ff] = dot(in_rows, w_gate[...]).astype(BF).reshape(shape)
        part[p, :, :, ff : 2 * ff] = dot(in_rows, w_up[...]).astype(BF).reshape(shape)
        part[p, :, :, 2 * ff :] = dot(in_grads, w_down[...], NT).astype(BF).reshape(shape)
        goal = (z + 4) % NZ
        half = block // 2
        send(
            part.at[p, goal, 0:half], minus.at[p, 0, 0:half], "scatter", rs_r.at[p, 0, 0], zdown
        )
        send(part.at[p, goal, half:], plus.at[p, 0, half:], "scatter", rs_r.at[p, 1, 0], zup)

    def scatter_down(p, s):
        low = (z + 4 + s) % NZ
        half = block // 2
        if s == 1:
            arrived(minus.at[p, 0, 0:half], rs_r.at[p, 0, 0], zup)
            part[p, low, 0:half] = add(part[p, low, 0:half], minus[p, 0, 0:half])
        else:
            arrived(minus.at[p, s - 1], rs_r.at[p, 0, s - 1], zup)
            part[p, low] = add(part[p, low], minus[p, s - 1])
        send(part.at[p, low], minus.at[p, s], "scatter", rs_r.at[p, 0, s], zdown)

    def scatter_up(p, s):
        high = (z + 4 - s) % NZ
        half = block // 2
        if s == 1:
            arrived(plus.at[p, 0, half:], rs_r.at[p, 1, 0], zdown)
            part[p, high, half:] = add(part[p, high, half:], plus[p, 0, half:])
        else:
            arrived(plus.at[p, s - 1], rs_r.at[p, 1, s - 1], zdown)
            part[p, high] = add(part[p, high], plus[p, s - 1])
        send(part.at[p, high], plus.at[p, s], "scatter", rs_r.at[p, 1, s], zup)

    def hidden(p):
        arrived(minus.at[p, 3], rs_r.at[p, 0, 3], zup)
        arrived(plus.at[p, 3], rs_r.at[p, 1, 3], zdown)
        total = part[p, z].astype(F32) + minus[p, 3].astype(F32) + plus[p, 3].astype(F32)
        gate, lift, back = total[:, :ff], total[:, ff : 2 * ff], total[:, 2 * ff :]
        sigmoid = 1.0 / (1.0 + jnp.exp(-gate))
        active = gate * sigmoid
        value = active * lift
        mine = grads.at[p, z]
        mine[:, 0:ff] = (back * lift * sigmoid * (1.0 + gate * (1.0 - sigmoid))).astype(BF)
        mine[:, ff : 2 * ff] = (back * active).astype(BF)
        mine[:, 2 * ff :] = value.astype(BF)
        send(mine, mine, "gather", ag_r.at[p, 1, 0], zup)
        send(mine, mine, "gather", ag_r.at[p, 0, 0], zdown)
        terms = back * value
        high = terms.astype(BF)
        rest = (terms - high.astype(F32)).astype(BF)
        ones = jnp.ones((8, ff), BF)
        summed = dot(ones, high, NT) + dot(ones, rest, NT)
        tile_z[p : p + 1, 0:block] = summed[0:1]

    def gather_down(p, s):
        low = grads.at[p, (z + s) % NZ]
        arrived(low, ag_r.at[p, 0, s - 1], zup)
        if s == 3:
            low = grads.at[p, (z + s) % NZ, 0 : block // 2]
        send(low, low, "gather", ag_r.at[p, 0, s], zdown)

    def gather_up(p, s):
        high = grads.at[p, (z - s + NZ) % NZ]
        arrived(high, ag_r.at[p, 1, s - 1], zdown)
        if s == 3:
            high = grads.at[p, (z - s + NZ) % NZ, block // 2 :]
        send(high, high, "gather", ag_r.at[p, 1, s], zup)

    gathered = set()

    def all_gathered(p):
        if p not in gathered:
            gathered.add(p)
            half = block // 2
            arrived(grads.at[p, (z + 4) % NZ, 0:half], ag_r.at[p, 0, 3], zup)
            arrived(grads.at[p, (z + 4) % NZ, half:], ag_r.at[p, 1, 3], zdown)

    def tokens(p):
        all_gathered(p)
        for k in (1, 0):
            both = grads[p, k * NY : (k + 1) * NY].reshape(NY * block, 3 * ff)
            value = dot(both[:, :ff], w_gate[...], NT) + dot(both[:, ff : 2 * ff], w_up[...], NT)
            tokens_out[p, k] = value.astype(BF).reshape(NY, block, width)
            if k == 1:
                send(tokens_out.at[p, 1], sibling_in.at[p], "terms", t_r.at[p], other)

    stores = [
        pltpu.make_async_copy(src, dst, out_s.at[i])
        for i, (src, dst) in enumerate(
            ((grad_gate, grad_gate_out), (grad_up, grad_up_out), (grad_down, grad_down_out))
        )
    ]

    def weights(p):
        all_gathered(p)
        both = grads[p].reshape(count, 3 * ff)
        in_rows = rows[p, 0].reshape(count, width)
        in_grads = rows[p, 1].reshape(count, width)
        gate = dot(in_rows, both[:, :ff], TN)
        lift = dot(in_rows, both[:, ff : 2 * ff], TN)
        drop = dot(both[:, 2 * ff :], in_grads, TN)
        if p == weight_groups[0]:
            acc_gate[...], acc_up[...], acc_down[...] = gate, lift, drop
        elif p != weight_groups[-1]:
            acc_gate[...] += gate
            acc_up[...] += lift
            acc_down[...] += drop
        else:
            grad_gate[...] = (acc_gate[...] + gate).astype(BF)
            grad_up[...] = (acc_up[...] + lift).astype(BF)
            grad_down[...] = (acc_down[...] + drop).astype(BF)
            for copy in stores:
                copy.start()

    def join(p):
        half = block // 2
        arrived(sibling_in.at[p], t_r.at[p], other)
        tokens_out[p, 0] = add(tokens_out[p, 0], sibling_in[p])
        send(tokens_out.at[p, 0, 3, 0:half], far_in.at[p, 0], "sums", yr_r.at[p, 0], up)
        send(tokens_out.at[p, 0, 3, half:], far_in.at[p, 1], "sums", yr_r.at[p, 1], down)

    def relay_up(p):
        half = block // 2
        arrived(far_in.at[p, 0], yr_r.at[p, 0], down)
        tokens_out[p, 0, 1, 0:half] = add(tokens_out[p, 0, 1, 0:half], far_in[p, 0])
        send(tokens_out.at[p, 0, 1], near_in.at[p, 0], "sums", yr_r.at[p, 2], up)

    def relay_down(p):
        half = block // 2
        arrived(far_in.at[p, 1], yr_r.at[p, 1], up)
        tokens_out[p, 0, 2, half:] = add(tokens_out[p, 0, 2, half:], far_in[p, 1])
        send(tokens_out.at[p, 0, 2], near_in.at[p, 1], "sums", yr_r.at[p, 3], down)

    def finish(p):
        arrived(near_in.at[p, 0], yr_r.at[p, 2], down)
        arrived(near_in.at[p, 1], yr_r.at[p, 3], up)
        value = tokens_out[p, 0, 0].astype(F32) + near_in[p, 0].astype(F32) + near_in[p, 1].astype(F32)
        final[p * NZ : (p + 1) * NZ] = value.reshape(NZ, CAP, width).astype(BF)
        for dz in steps_z:
            if (dz, p) != (0, 0):
                send(final.at[p * NZ + (z + dz) % NZ], table.at[z, x], "back", back_r, at(dz, p))
            else:
                table[z, x] = final[z]

    others_z = range(1, NZ)

    def router_start():
        for dz in others_z:
            send(tile_z, tile_zin.at[z], "rz", router_r.at[0], at(dz))
        tile_zin[z] = tile_z[...]

    def three_parts(value):
        top = value.astype(BF)
        middle = (value - top.astype(F32)).astype(BF)
        low = (value - top.astype(F32) - middle.astype(F32)).astype(BF)
        return top, middle, low

    def moved(value, source, goal):
        move = jnp.where(source & goal, 1.0, 0.0).astype(BF)
        top, middle, low = three_parts(value)
        return dot(top, move) + dot(middle, move) + dot(low, move)

    row = lax.broadcasted_iota(jnp.int32, (128, 128), 0)
    column = lax.broadcasted_iota(jnp.int32, (128, 128), 1)
    in_slot = jnp.bitwise_and(row, CAP - 1)

    def router_local():
        arrived(tile_zin.at[1:NZ], router_r.at[0], zup)
        total = jnp.zeros((8, 128), F32)
        inside = lax.broadcasted_iota(jnp.int32, (8, 128), 1) < block
        for p in range(NX):
            value = jnp.concatenate([tile_zin[b, p : p + 1, :] for b in range(NZ)], axis=0)
            value = jnp.where(inside, value, 0.0)
            total = total + moved(value, jnp.right_shift(row, 3) == z, column == p * CAP + in_slot)
        tile[...] = total
        for k, g in around:
            i = NY * k + g
            send(tile, tile_in.at[i], "ry", router_r.at[1], at(dy=GROUP_Y[g], dc=k))

    def router_x():
        summed = tile[0:1, :]
        arrived(tile_in.at[1 : NY * NC], router_r.at[1], other)
        for k, g in around:
            i = NY * k + g
            summed = summed + tile_in[i, i : i + 1, :]
        wide = jnp.broadcast_to(summed, (8, 128))
        for dx in range(NX):
            tile_x[dx] = moved(wide, jnp.right_shift(row, 3) == dx, column == x * CAP + in_slot)
        router[x] = tile_x[0]
        for dx in range(1, NX):
            send(tile_x.at[dx], router.at[x], "rx", router_r.at[2], at(dx=dx))

    todo = {
        "take": take, "products": products, "hidden": hidden, "tokens": tokens, "weights": weights,
        "pass_tokens": pass_tokens, "pass_grads": pass_grads,
        "near_grads": functools.partial(keep, g=1, h=1),
        "near_tokens": functools.partial(keep, g=2, h=0),
        "far_tokens": functools.partial(keep, g=3, h=0),
        "far_grads": functools.partial(keep, g=3, h=1),
        "join": join, "relay_up": relay_up, "relay_down": relay_down, "finish": finish,
    }
    for s in (1, 2, 3):
        todo[f"scatter_down_{s}"] = functools.partial(scatter_down, s=s)
        todo[f"scatter_up_{s}"] = functools.partial(scatter_up, s=s)
        todo[f"gather_down_{s}"] = functools.partial(gather_down, s=s)
        todo[f"gather_up_{s}"] = functools.partial(gather_up, s=s)
    plan = sorted(
        (place, stage, p) for stage, *places in STAGES for place, p in zip(places, ORDER)
    )
    weight_groups = [p for _, stage, p in plan if stage == "weights"]
    last = {stage: max(places) for stage, *places in STAGES}
    after = {
        last["hidden"]: router_start, last["gather_down_2"]: router_local, last["tokens"]: router_x
    }
    for place, stage, p in plan:
        todo[stage](p)
        if place in after:
            after[place]()

    arrived(tile_x.at[1:NX], router_r.at[2], at(dx=1))
    arrived(final.at[1:], back_r, zup)
    for copy in stores:
        copy.wait()
    all_sent("a2a", packed.at[1:])
    all_sent("y", rows.at[:, :, 0, 1:])
    all_sent("sibling", rows.at[:, :, 1])
    all_sent("scatter", part.at[:, 1:])
    all_sent("gather", grads.at[:, 1:])
    all_sent("terms", sibling_in)
    all_sent("sums", tokens_out.at[:, 0, 1:])
    all_sent("back", final.at[1:])
    all_sent("rz", tile_zin.at[1:])
    all_sent("ry", tile_in.at[1:])
    all_sent("rx", tile_x.at[1:])


def experts(routes, probs, tokens, cotangent, w_gate, w_up, w_down):
    width, ff = w_gate.shape
    count = tokens.shape[0]
    block = NZ * CAP
    vmem = pl.BlockSpec(memory_space=pltpu.VMEM)
    free = pl.BlockSpec(memory_space=pl.ANY)
    dma = lambda *shape: pltpu.SemaphoreType.DMA(shape)
    flops = 2 * 8 * NX * NC * NY * block * width * ff
    return pl.pallas_call(
        expert_kernel,
        out_shape=(
            jax.ShapeDtypeStruct((NX * CAP, count), BF),
            jax.ShapeDtypeStruct((NZ, NX, CAP, width), BF),
            jax.ShapeDtypeStruct((NX, 8, 128), F32),
            jax.ShapeDtypeStruct((width, ff), BF),
            jax.ShapeDtypeStruct((width, ff), BF),
            jax.ShapeDtypeStruct((ff, width), BF),
        ),
        in_specs=[vmem] * 2 + [free] * 5,
        out_specs=(vmem,) * 3 + (free,) * 3,
        scratch_shapes=[
            pltpu.VMEM((NZ, 2, count, width), BF),
            pltpu.VMEM((width, ff), BF),
            pltpu.VMEM((width, ff), BF),
            pltpu.VMEM((ff, width), BF),
            pltpu.VMEM((width, ff), BF),
            pltpu.VMEM((width, ff), BF),
            pltpu.VMEM((ff, width), BF),
            pltpu.VMEM((NZ * NX, 2 * CAP, width), BF),
            pltpu.VMEM((NX, NZ, 2 * CAP, width), BF),
            pltpu.VMEM((NX, 2, NC, NY, block, width), BF),
            pltpu.VMEM((NX, NZ, block, 3 * ff), BF),
            pltpu.VMEM((NX, 4, block, 3 * ff), BF),
            pltpu.VMEM((NX, 4, block, 3 * ff), BF),
            pltpu.VMEM((NX, NZ, block, 3 * ff), BF),
            pltpu.VMEM((NX, NC, NY, block, width), BF),
            pltpu.VMEM((NX, NY, block, width), BF),
            pltpu.VMEM((NX, 2, block, width), BF),
            pltpu.VMEM((NX, 2, block // 2, width), BF),
            pltpu.VMEM((NX * NZ, CAP, width), BF),
            pltpu.VMEM((width, ff), F32),
            pltpu.VMEM((width, ff), F32),
            pltpu.VMEM((ff, width), F32),
            pltpu.VMEM((8, 128), F32),
            pltpu.VMEM((NZ, 8, 128), F32),
            pltpu.VMEM((8, 128), F32),
            pltpu.VMEM((8, 8, 128), F32),
            pltpu.VMEM((NX, 8, 128), F32),
            dma(11), dma(NX), dma(NX, 3, 2), dma(NX), dma(NX, 2, 4), dma(NX, 2, 4), dma(NX), dma(NX, 4),
            pltpu.SemaphoreType.DMA, dma(NZ), dma(3), dma(3), dma(3),
        ],
        compiler_params=pltpu.CompilerParams(
            collective_id=0, has_side_effects=True, vmem_limit_bytes=56 * MIB
        ),
        cost_estimate=pl.CostEstimate(flops=flops, bytes_accessed=16 * MIB, transcendentals=0),
    )(routes, probs, tokens, cotangent, w_gate, w_up, w_down)


def per_device(tokens, cotangent, routes, probs, w_gate, w_up, w_down):
    routes, probs = routes.T, probs.T
    choice, table, router, gate, lift, drop = experts(
        routes, probs, tokens, cotangent, w_gate[0], w_up[0], w_down[0]
    )
    token_grad, router_grad, gate, lift, drop = unpack(
        routes, probs, choice, table, router, gate, lift, drop
    )
    return token_grad, router_grad.T, gate, lift, drop


def solution(mesh):
    split = P(("dp", "node", "local"), None)
    specs = (P("node", "dp", "local"), P("node", "dp", "local"), P("node", "local", "dp"))
    return jax.shard_map(
        per_device,
        mesh=mesh,
        in_specs=(split,) * 4 + specs,
        out_specs=(split,) * 2 + specs,
        check_vma=False,
    )
```

```python
import functools

import jax
import jax.numpy as jnp
from jax import lax
from jax.experimental import pallas as pl
from jax.experimental.pallas import tpu as pltpu
from jax.sharding import PartitionSpec as P

NZ, NX, NY, NC = 8, 4, 4, 2
CAP = 8
BF = jnp.bfloat16
F32 = jnp.float32
MESH = pl.DeviceIdType.MESH
NN = (((1,), (0,)), ((), ()))
NT = (((1,), (1,)), ((), ()))
TN = (((0,), (0,)), ((), ()))
MIB = 1024 * 1024


def dot(a, b, dims=NN):
    return lax.dot_general(a, b, dims, preferred_element_type=F32)


def choose(routes, probs):
    top, rows = routes.shape
    slots = NX * CAP
    place = lax.broadcasted_iota(jnp.int32, (slots, rows), 0)
    expert = jnp.right_shift(place, 3)
    hit = jnp.zeros((slots, rows), F32)
    scale = jnp.zeros((slots, rows), F32)
    for k in range(top):
        same = routes[k : k + 1, :] == expert
        hit = jnp.where(same, 1.0, hit)
        scale = jnp.where(same, probs[k : k + 1, :], scale)
    before = lax.broadcasted_iota(jnp.int32, (rows, rows), 0) < lax.broadcasted_iota(
        jnp.int32, (rows, rows), 1
    )
    earlier = dot(hit.astype(BF), jnp.where(before, 1.0, 0.0).astype(BF))
    slot = jnp.bitwise_and(place, CAP - 1).astype(F32)
    mark = jnp.where(earlier == slot, hit, 0.0)
    return mark.astype(BF), (mark * scale).astype(BF)


def unpack_kernel(
    routes, probs, choice, table, router, gate_in, up_in, down_in,
    token_grad, router_grad, gate_out, up_out, down_out,
    slots_v, result, gate_v, up_v, down_v, result_s, load_s, grad_s,
):
    top, rows = routes.shape
    slots = NX * CAP
    width = table.shape[3]
    copies = []

    def copy(src, dst, sem):
        started = pltpu.make_async_copy(src, dst, sem)
        started.start()
        copies.append(started)

    through = ((gate_in, gate_v, gate_out), (up_in, up_v, up_out), (down_in, down_v, down_out))
    loads = [pltpu.make_async_copy(src, v, load_s.at[i]) for i, (src, v, _) in enumerate(through)]
    for load in loads:
        load.start()
    chosen = choice[...]
    for d in range(NZ):
        rows_in = table[d].astype(F32).reshape(slots, width).astype(BF)
        slots_v[:, d * width : (d + 1) * width] = rows_in
    some = result.shape[1]
    for r in range(result.shape[0]):
        result[r] = dot(chosen[:, r * some : (r + 1) * some], slots_v[...], TN).astype(BF)
        copy(result.at[r], token_grad.at[r * some : (r + 1) * some], result_s.at[r])

    for i, (_, v, dst) in enumerate(through):
        loads[i].wait()
        copy(v, dst.at[0], grad_s.at[i])

    values = (router[0] + router[1] + router[2] + router[3])[0:1, 0:slots]
    row, column = (lax.broadcasted_iota(jnp.int32, (slots, slots), i) for i in range(2))
    values = jnp.sum(jnp.where(row == column, values, 0.0), axis=1, keepdims=True)
    spread = chosen.astype(F32) * values
    expert = jnp.right_shift(lax.broadcasted_iota(jnp.int32, (slots, rows), 0), 3)
    named = routes[...]
    place = lax.broadcasted_iota(jnp.int32, (top, rows), 0)
    total = jnp.zeros((top, rows), F32)
    for k in range(top):
        mine = jnp.where(named[k : k + 1, :] == expert, spread, 0.0)
        total = jnp.where(place == k, jnp.sum(mine, axis=0, keepdims=True), total)
    router_grad[...] = total / probs[...].astype(F32)
    for started in copies:
        started.wait()


def unpack(routes, probs, choice, table, router, gate, lift, drop):
    top, rows = routes.shape
    part = table.shape[3]
    width, ff = gate.shape
    vmem = pl.BlockSpec(memory_space=pltpu.VMEM)
    free = pl.BlockSpec(memory_space=pl.ANY)
    return pl.pallas_call(
        unpack_kernel,
        out_shape=(
            jax.ShapeDtypeStruct((rows, NZ * part), BF),
            jax.ShapeDtypeStruct((top, rows), F32),
            jax.ShapeDtypeStruct((1, width, ff), BF),
            jax.ShapeDtypeStruct((1, width, ff), BF),
            jax.ShapeDtypeStruct((1, ff, width), BF),
        ),
        in_specs=[vmem] * 5 + [free] * 3,
        out_specs=(free, vmem, free, free, free),
        scratch_shapes=[
            pltpu.VMEM((NX * CAP, NZ * part), BF),
            pltpu.VMEM((4, rows // 4, NZ * part), BF),
            pltpu.VMEM((width, ff), BF),
            pltpu.VMEM((width, ff), BF),
            pltpu.VMEM((ff, width), BF),
            pltpu.SemaphoreType.DMA((NZ,)),
            pltpu.SemaphoreType.DMA((3,)),
            pltpu.SemaphoreType.DMA((3,)),
        ],
        compiler_params=pltpu.CompilerParams(vmem_limit_bytes=58 * MIB),
    )(routes, probs, choice, table, router, gate, lift, drop)


GROUP_Y = (0, 1, NY - 1, 2)
ORDER = (0, 1, 3, 2)

STAGES = (
    ("take", 0, 3, 13, 23),
    ("pass_tokens", 1, 9, 19, 34),
    ("pass_grads", 2, 10, 22, 35),
    ("near_grads", 5, 11, 24, 46),
    ("near_tokens", 4, 12, 27, 38),
    ("far_tokens", 6, 16, 31, 41),
    ("far_grads", 7, 17, 30, 42),
    ("products", 8, 18, 36, 48),
    ("scatter_down_1", 14, 25, 43, 52),
    ("scatter_up_1", 15, 26, 44, 56),
    ("scatter_down_2", 21, 32, 53, 59),
    ("scatter_up_2", 20, 33, 54, 62),
    ("scatter_down_3", 28, 39, 61, 65),
    ("scatter_up_3", 29, 40, 60, 67),
    ("hidden", 37, 49, 68, 73),
    ("gather_down_1", 45, 55, 74, 77),
    ("gather_up_1", 47, 58, 75, 78),
    ("gather_down_2", 50, 63, 81, 83),
    ("gather_up_2", 51, 64, 82, 84),
    ("gather_down_3", 57, 70, 87, 91),
    ("gather_up_3", 66, 71, 89, 92),
    ("tokens", 72, 76, 93, 94),
    ("weights", 69, 104, 106, 107),
    ("join", 80, 79, 95, 97),
    ("relay_up", 85, 88, 98, 102),
    ("relay_down", 86, 90, 99, 101),
    ("finish", 96, 100, 103, 105),
)


def expert_kernel(
    routes, probs, tokens_in, cotangent_in, gate_in, up_in, down_in,
    choice, table, router, grad_gate_out, grad_up_out, grad_down_out,
    inputs, w_gate, w_up, w_down, grad_gate, grad_up, grad_down, packed,
    land, rows, part, minus, plus, grads, tokens_out, sibling_in, near_in, far_in, final,
    acc_gate, acc_up, acc_down, tile_z, tile_zin, tile, tile_in, tile_x,
    sent, a2a_r, y_r, sib_r, rs_r, ag_r, t_r, yr_r, back_r, in_s, w_s, out_s, router_r,
):
    z, x, loc = lax.axis_index("dp"), lax.axis_index("node"), lax.axis_index("local")
    y, c = loc // NC, loc % NC
    width = packed.shape[2]
    ff = w_gate.shape[1]
    block = NZ * CAP
    count = NC * NY * block

    def at(dz=0, dx=0, dy=0, dc=0):
        return {
            "dp": (z + dz) % NZ,
            "node": (x + dx) % NX,
            "local": ((y + dy) % NY) * NC + (c + dc) % NC,
        }

    steps_z = (4, 3, 5, 2, 6, 1, 7, 0)
    for dz in steps_z:
        start = pl.multiple_of((z + dz) % NZ * width, 128)
        for i, src in enumerate((tokens_in, cotangent_in)):
            pltpu.make_async_copy(
                src.at[:, pl.ds(start, width)], inputs.at[dz, i], in_s.at[dz]
            ).start()
    weight_loads = [
        pltpu.make_async_copy(src, dst, w_s.at[i])
        for i, (src, dst) in enumerate(((gate_in, w_gate), (up_in, w_up), (down_in, w_down)))
    ]
    for load in weight_loads:
        load.start()

    kinds = ("a2a", "y", "sibling", "scatter", "gather", "terms", "sums", "back", "rz", "ry", "rx")

    def send(src, dst, kind, recv_sem, device):
        pltpu.make_async_remote_copy(
            src_ref=src, dst_ref=dst, send_sem=sent.at[kinds.index(kind)], recv_sem=recv_sem,
            device_id=device, device_id_type=MESH,
        ).start()

    def all_sent(kind, same_bytes):
        pltpu.make_async_remote_copy(
            src_ref=same_bytes, dst_ref=same_bytes, send_sem=sent.at[kinds.index(kind)],
            recv_sem=back_r, device_id=at(dz=1), device_id_type=MESH,
        ).wait_send()

    def arrived(dst, recv_sem, device):
        pltpu.make_async_remote_copy(
            src_ref=dst, dst_ref=dst, send_sem=recv_sem, recv_sem=recv_sem,
            device_id=device, device_id_type=MESH,
        ).wait_recv()

    def add(a, b):
        return (a.astype(F32) + b.astype(F32)).astype(BF)

    plane = [(dz, p) for p in ORDER for dz in steps_z if (dz, p) != (0, 0)]
    around = [(k, g) for k in range(NC) for g in range(NY) if (k, g) != (0, 0)]

    barrier = pltpu.get_barrier_semaphore()
    for dz, dx in plane:
        pl.semaphore_signal(barrier, inc=1, device_id=at(dz, dx), device_id_type=MESH)
    for k, g in around:
        pl.semaphore_signal(barrier, inc=1, device_id=at(dy=GROUP_Y[g], dc=k), device_id_type=MESH)
    pick, pick_scaled = choose(routes[...], probs[...].astype(F32))
    choice[...] = pick
    pl.semaphore_wait(barrier, len(plane) + len(around))

    def give(dz, p):
        if (dz, p) == (0, 0):
            land[0, z] = packed[x]
            return
        dx = (-p) % NX
        send(packed.at[dz * NX + (x + dx) % NX], land.at[p, z], "a2a", a2a_r.at[p], at(dz, dx))

    for dz in steps_z:
        pltpu.make_async_copy(inputs.at[dz], inputs.at[dz], in_s.at[dz]).wait()
        rows_x = dot(pick, inputs[dz, 0]).reshape(NX, CAP, width)
        rows_c = dot(pick_scaled, inputs[dz, 1]).reshape(NX, CAP, width)
        packed[dz * NX : (dz + 1) * NX] = jnp.concatenate([rows_x, rows_c], axis=1).astype(BF)
        give(dz, ORDER[0])
    for p in ORDER[1:]:
        for dz in steps_z:
            give(dz, p)
    for load in weight_loads:
        load.wait()

    up, down, other = at(dy=1), at(dy=NY - 1), at(dc=1)
    zup, zdown = at(dz=1), at(dz=NZ - 1)

    def take(p):
        arrived(land.at[p, (1 if p == 0 else 0) : NZ], a2a_r.at[p], zup)
        mixed = land[p].astype(F32)
        rows[p, 0, 0, 0] = mixed[:, :CAP].reshape(block, width).astype(BF)
        rows[p, 1, 0, 0] = mixed[:, CAP:].reshape(block, width).astype(BF)
        for h in range(2):
            send(rows.at[p, h, 0, 0], rows.at[p, h, 0, 1], "y", y_r.at[p, 0, h], down)
            send(rows.at[p, 1 - h, 0, 0], rows.at[p, 1 - h, 0, 2], "y", y_r.at[p, 1, 1 - h], up)
        to_sibling(p, 0, 1)

    def to_sibling(p, first, last):
        send(
            rows.at[p, :, 0, first:last], rows.at[p, :, 1, first:last], "sibling", sib_r.at[p], other
        )

    left = {p: {1: 4, 3: 2} for p in ORDER}

    def from_y(p, g, h):
        arrived(rows.at[p, h, 0, g], y_r.at[p, g - 1, h], up)
        first, last = (3, 4) if g == 3 else (1, 3)
        left[p][first] -= 1
        if left[p][first] == 0:
            to_sibling(p, first, last)

    def pass_tokens(p):
        from_y(p, 1, 0)
        send(rows.at[p, 0, 0, 1], rows.at[p, 0, 0, 3], "y", y_r.at[p, 2, 0], down)

    def pass_grads(p):
        from_y(p, 2, 1)
        send(rows.at[p, 1, 0, 2], rows.at[p, 1, 0, 3], "y", y_r.at[p, 2, 1], up)

    def products(p):
        arrived(rows.at[p, :, 1], sib_r.at[p], other)
        in_rows = rows[p, 0].reshape(count, width)
        in_grads = rows[p, 1].reshape(count, width)
        shape = (NZ, block, ff)
        part[p, :, :, 0:ff] = dot(in_rows, w_gate[...]).astype(BF).reshape(shape)
        part[p, :, :, ff : 2 * ff] = dot(in_rows, w_up[...]).astype(BF).reshape(shape)
        part[p, :, :, 2 * ff :] = dot(in_grads, w_down[...], NT).astype(BF).reshape(shape)
        goal = (z + 4) % NZ
        half = block // 2
        send(
            part.at[p, goal, 0:half], minus.at[p, 0, 0:half], "scatter", rs_r.at[p, 0, 0], zdown
        )
        send(part.at[p, goal, half:], plus.at[p, 0, half:], "scatter", rs_r.at[p, 1, 0], zup)

    def scatter_down(p, s):
        low = (z + 4 + s) % NZ
        half = block // 2
        if s == 1:
            arrived(minus.at[p, 0, 0:half], rs_r.at[p, 0, 0], zup)
            part[p, low, 0:half] = add(part[p, low, 0:half], minus[p, 0, 0:half])
        else:
            arrived(minus.at[p, s - 1], rs_r.at[p, 0, s - 1], zup)
            part[p, low] = add(part[p, low], minus[p, s - 1])
        send(part.at[p, low], minus.at[p, s], "scatter", rs_r.at[p, 0, s], zdown)

    def scatter_up(p, s):
        high = (z + 4 - s) % NZ
        half = block // 2
        if s == 1:
            arrived(plus.at[p, 0, half:], rs_r.at[p, 1, 0], zdown)
            part[p, high, half:] = add(part[p, high, half:], plus[p, 0, half:])
        else:
            arrived(plus.at[p, s - 1], rs_r.at[p, 1, s - 1], zdown)
            part[p, high] = add(part[p, high], plus[p, s - 1])
        send(part.at[p, high], plus.at[p, s], "scatter", rs_r.at[p, 1, s], zup)

    def hidden(p):
        arrived(minus.at[p, 3], rs_r.at[p, 0, 3], zup)
        arrived(plus.at[p, 3], rs_r.at[p, 1, 3], zdown)
        total = part[p, z].astype(F32) + minus[p, 3].astype(F32) + plus[p, 3].astype(F32)
        gate, lift, back = total[:, :ff], total[:, ff : 2 * ff], total[:, 2 * ff :]
        sigmoid = 1.0 / (1.0 + jnp.exp(-gate))
        active = gate * sigmoid
        value = active * lift
        mine = grads.at[p, z]
        mine[:, 0:ff] = (back * lift * sigmoid * (1.0 + gate * (1.0 - sigmoid))).astype(BF)
        mine[:, ff : 2 * ff] = (back * active).astype(BF)
        mine[:, 2 * ff :] = value.astype(BF)
        send(mine, mine, "gather", ag_r.at[p, 1, 0], zup)
        send(mine, mine, "gather", ag_r.at[p, 0, 0], zdown)
        terms = back * value
        high = terms.astype(BF)
        rest = (terms - high.astype(F32)).astype(BF)
        ones = jnp.ones((8, ff), BF)
        summed = dot(ones, high, NT) + dot(ones, rest, NT)
        tile_z[p : p + 1, 0:block] = summed[0:1]

    def gather_down(p, s):
        low = grads.at[p, (z + s) % NZ]
        arrived(low, ag_r.at[p, 0, s - 1], zup)
        if s == 3:
            low = grads.at[p, (z + s) % NZ, 0 : block // 2]
        send(low, low, "gather", ag_r.at[p, 0, s], zdown)

    def gather_up(p, s):
        high = grads.at[p, (z - s + NZ) % NZ]
        arrived(high, ag_r.at[p, 1, s - 1], zdown)
        if s == 3:
            high = grads.at[p, (z - s + NZ) % NZ, block // 2 :]
        send(high, high, "gather", ag_r.at[p, 1, s], zup)

    gathered = set()

    def all_gathered(p):
        if p not in gathered:
            gathered.add(p)
            half = block // 2
            arrived(grads.at[p, (z + 4) % NZ, 0:half], ag_r.at[p, 0, 3], zup)
            arrived(grads.at[p, (z + 4) % NZ, half:], ag_r.at[p, 1, 3], zdown)

    def tokens(p):
        all_gathered(p)
        for k in (1, 0):
            both = grads[p, k * NY : (k + 1) * NY].reshape(NY * block, 3 * ff)
            value = dot(both[:, :ff], w_gate[...], NT) + dot(both[:, ff : 2 * ff], w_up[...], NT)
            tokens_out[p, k] = value.astype(BF).reshape(NY, block, width)
            if k == 1:
                send(tokens_out.at[p, 1], sibling_in.at[p], "terms", t_r.at[p], other)

    stores = [
        pltpu.make_async_copy(src, dst, out_s.at[i])
        for i, (src, dst) in enumerate(
            ((grad_gate, grad_gate_out), (grad_up, grad_up_out), (grad_down, grad_down_out))
        )
    ]

    def weights(p):
        all_gathered(p)
        both = grads[p].reshape(count, 3 * ff)
        in_rows = rows[p, 0].reshape(count, width)
        in_grads = rows[p, 1].reshape(count, width)
        gate = dot(in_rows, both[:, :ff], TN)
        lift = dot(in_rows, both[:, ff : 2 * ff], TN)
        drop = dot(both[:, 2 * ff :], in_grads, TN)
        if p == weight_groups[0]:
            acc_gate[...], acc_up[...], acc_down[...] = gate, lift, drop
        elif p != weight_groups[-1]:
            acc_gate[...] += gate
            acc_up[...] += lift
            acc_down[...] += drop
        else:
            grad_gate[...] = (acc_gate[...] + gate).astype(BF)
            grad_up[...] = (acc_up[...] + lift).astype(BF)
            grad_down[...] = (acc_down[...] + drop).astype(BF)
            for copy in stores:
                copy.start()

    def join(p):
        half = block // 2
        arrived(sibling_in.at[p], t_r.at[p], other)
        tokens_out[p, 0] = add(tokens_out[p, 0], sibling_in[p])
        send(tokens_out.at[p, 0, 3, 0:half], far_in.at[p, 0], "sums", yr_r.at[p, 0], up)
        send(tokens_out.at[p, 0, 3, half:], far_in.at[p, 1], "sums", yr_r.at[p, 1], down)

    def relay_up(p):
        half = block // 2
        arrived(far_in.at[p, 0], yr_r.at[p, 0], down)
        tokens_out[p, 0, 1, 0:half] = add(tokens_out[p, 0, 1, 0:half], far_in[p, 0])
        send(tokens_out.at[p, 0, 1], near_in.at[p, 0], "sums", yr_r.at[p, 2], up)

    def relay_down(p):
        half = block // 2
        arrived(far_in.at[p, 1], yr_r.at[p, 1], up)
        tokens_out[p, 0, 2, half:] = add(tokens_out[p, 0, 2, half:], far_in[p, 1])
        send(tokens_out.at[p, 0, 2], near_in.at[p, 1], "sums", yr_r.at[p, 3], down)

    def finish(p):
        arrived(near_in.at[p, 0], yr_r.at[p, 2], down)
        arrived(near_in.at[p, 1], yr_r.at[p, 3], up)
        value = tokens_out[p, 0, 0].astype(F32) + near_in[p, 0].astype(F32) + near_in[p, 1].astype(F32)
        final[p * NZ : (p + 1) * NZ] = value.reshape(NZ, CAP, width).astype(BF)
        for dz in steps_z:
            if (dz, p) != (0, 0):
                send(final.at[p * NZ + (z + dz) % NZ], table.at[z, x], "back", back_r, at(dz, p))
            else:
                table[z, x] = final[z]

    others_z = range(1, NZ)

    def router_start():
        for dz in others_z:
            send(tile_z, tile_zin.at[z], "rz", router_r.at[0], at(dz))
        tile_zin[z] = tile_z[...]

    def three_parts(value):
        top = value.astype(BF)
        middle = (value - top.astype(F32)).astype(BF)
        low = (value - top.astype(F32) - middle.astype(F32)).astype(BF)
        return top, middle, low

    def moved(value, source, goal):
        move = jnp.where(source & goal, 1.0, 0.0).astype(BF)
        top, middle, low = three_parts(value)
        return dot(top, move) + dot(middle, move) + dot(low, move)

    row = lax.broadcasted_iota(jnp.int32, (128, 128), 0)
    column = lax.broadcasted_iota(jnp.int32, (128, 128), 1)
    in_slot = jnp.bitwise_and(row, CAP - 1)

    def router_local():
        arrived(tile_zin.at[1:NZ], router_r.at[0], zup)
        total = jnp.zeros((8, 128), F32)
        inside = lax.broadcasted_iota(jnp.int32, (8, 128), 1) < block
        for p in range(NX):
            value = jnp.concatenate([tile_zin[b, p : p + 1, :] for b in range(NZ)], axis=0)
            value = jnp.where(inside, value, 0.0)
            total = total + moved(value, jnp.right_shift(row, 3) == z, column == p * CAP + in_slot)
        tile[...] = total
        for k, g in around:
            i = NY * k + g
            send(tile, tile_in.at[i], "ry", router_r.at[1], at(dy=GROUP_Y[g], dc=k))

    def router_x():
        summed = tile[0:1, :]
        arrived(tile_in.at[1 : NY * NC], router_r.at[1], other)
        for k, g in around:
            i = NY * k + g
            summed = summed + tile_in[i, i : i + 1, :]
        wide = jnp.broadcast_to(summed, (8, 128))
        for dx in range(NX):
            tile_x[dx] = moved(wide, jnp.right_shift(row, 3) == dx, column == x * CAP + in_slot)
        router[x] = tile_x[0]
        for dx in range(1, NX):
            send(tile_x.at[dx], router.at[x], "rx", router_r.at[2], at(dx=dx))

    todo = {
        "take": take, "products": products, "hidden": hidden, "tokens": tokens, "weights": weights,
        "pass_tokens": pass_tokens, "pass_grads": pass_grads,
        "near_grads": functools.partial(from_y, g=1, h=1),
        "near_tokens": functools.partial(from_y, g=2, h=0),
        "far_tokens": functools.partial(from_y, g=3, h=0),
        "far_grads": functools.partial(from_y, g=3, h=1),
        "join": join, "relay_up": relay_up, "relay_down": relay_down, "finish": finish,
    }
    for s in (1, 2, 3):
        todo[f"scatter_down_{s}"] = functools.partial(scatter_down, s=s)
        todo[f"scatter_up_{s}"] = functools.partial(scatter_up, s=s)
        todo[f"gather_down_{s}"] = functools.partial(gather_down, s=s)
        todo[f"gather_up_{s}"] = functools.partial(gather_up, s=s)
    plan = sorted(
        (place, stage, p) for stage, *places in STAGES for place, p in zip(places, ORDER)
    )
    weight_groups = [p for _, stage, p in plan if stage == "weights"]
    last = {stage: max(places) for stage, *places in STAGES}
    after = {
        last["hidden"]: router_start, last["gather_down_2"]: router_local, last["tokens"]: router_x
    }
    for place, stage, p in plan:
        todo[stage](p)
        if place in after:
            after[place]()

    arrived(tile_x.at[1:NX], router_r.at[2], at(dx=1))
    arrived(final.at[1:], back_r, zup)
    for copy in stores:
        copy.wait()
    all_sent("a2a", packed.at[1:])
    all_sent("y", rows.at[:, :, 0, 1:])
    all_sent("sibling", rows.at[:, :, 1])
    all_sent("scatter", part.at[:, 1:])
    all_sent("gather", grads.at[:, 1:])
    all_sent("terms", sibling_in)
    all_sent("sums", tokens_out.at[:, 0, 1:])
    all_sent("back", final.at[1:])
    all_sent("rz", tile_zin.at[1:])
    all_sent("ry", tile_in.at[1:])
    all_sent("rx", tile_x.at[1:])


def experts(routes, probs, tokens, cotangent, w_gate, w_up, w_down):
    width, ff = w_gate.shape
    count = tokens.shape[0]
    block = NZ * CAP
    vmem = pl.BlockSpec(memory_space=pltpu.VMEM)
    free = pl.BlockSpec(memory_space=pl.ANY)
    dma = lambda *shape: pltpu.SemaphoreType.DMA(shape)
    flops = 2 * 8 * NX * NC * NY * block * width * ff
    return pl.pallas_call(
        expert_kernel,
        out_shape=(
            jax.ShapeDtypeStruct((NX * CAP, count), BF),
            jax.ShapeDtypeStruct((NZ, NX, CAP, width), BF),
            jax.ShapeDtypeStruct((NX, 8, 128), F32),
            jax.ShapeDtypeStruct((width, ff), BF),
            jax.ShapeDtypeStruct((width, ff), BF),
            jax.ShapeDtypeStruct((ff, width), BF),
        ),
        in_specs=[vmem] * 2 + [free] * 5,
        out_specs=(vmem,) * 3 + (free,) * 3,
        scratch_shapes=[
            pltpu.VMEM((NZ, 2, count, width), BF),
            pltpu.VMEM((width, ff), BF),
            pltpu.VMEM((width, ff), BF),
            pltpu.VMEM((ff, width), BF),
            pltpu.VMEM((width, ff), BF),
            pltpu.VMEM((width, ff), BF),
            pltpu.VMEM((ff, width), BF),
            pltpu.VMEM((NZ * NX, 2 * CAP, width), BF),
            pltpu.VMEM((NX, NZ, 2 * CAP, width), BF),
            pltpu.VMEM((NX, 2, NC, NY, block, width), BF),
            pltpu.VMEM((NX, NZ, block, 3 * ff), BF),
            pltpu.VMEM((NX, 4, block, 3 * ff), BF),
            pltpu.VMEM((NX, 4, block, 3 * ff), BF),
            pltpu.VMEM((NX, NZ, block, 3 * ff), BF),
            pltpu.VMEM((NX, NC, NY, block, width), BF),
            pltpu.VMEM((NX, NY, block, width), BF),
            pltpu.VMEM((NX, 2, block, width), BF),
            pltpu.VMEM((NX, 2, block // 2, width), BF),
            pltpu.VMEM((NX * NZ, CAP, width), BF),
            pltpu.VMEM((width, ff), F32),
            pltpu.VMEM((width, ff), F32),
            pltpu.VMEM((ff, width), F32),
            pltpu.VMEM((8, 128), F32),
            pltpu.VMEM((NZ, 8, 128), F32),
            pltpu.VMEM((8, 128), F32),
            pltpu.VMEM((8, 8, 128), F32),
            pltpu.VMEM((NX, 8, 128), F32),
            dma(11), dma(NX), dma(NX, 3, 2), dma(NX), dma(NX, 2, 4), dma(NX, 2, 4), dma(NX), dma(NX, 4),
            pltpu.SemaphoreType.DMA, dma(NZ), dma(3), dma(3), dma(3),
        ],
        compiler_params=pltpu.CompilerParams(
            collective_id=0, has_side_effects=True, vmem_limit_bytes=56 * MIB
        ),
        cost_estimate=pl.CostEstimate(flops=flops, bytes_accessed=16 * MIB, transcendentals=0),
    )(routes, probs, tokens, cotangent, w_gate, w_up, w_down)


def per_device(tokens, cotangent, routes, probs, w_gate, w_up, w_down):
    routes, probs = routes.T, probs.T
    choice, table, router, gate, lift, drop = experts(
        routes, probs, tokens, cotangent, w_gate[0], w_up[0], w_down[0]
    )
    token_grad, router_grad, gate, lift, drop = unpack(
        routes, probs, choice, table, router, gate, lift, drop
    )
    return token_grad, router_grad.T, gate, lift, drop


def solution(mesh):
    split = P(("dp", "node", "local"), None)
    specs = (P("node", "dp", "local"), P("node", "dp", "local"), P("node", "local", "dp"))
    return jax.shard_map(
        per_device,
        mesh=mesh,
        in_specs=(split,) * 4 + specs,
        out_specs=(split,) * 2 + specs,
        check_vma=False,
    )
```
